32 devices in a mesh: layer: 2 (over core), row: 16 (over z, y, x).
Axes of the slice: x: 2, y: 2, z: 4, core: 2. Of those that a mesh axis runs over, the one named last changes fastest.
Arguments:
- residual: float32 [2, 2, 16, 1024, 192], P(None, None, 'layer', 'row'), may hold values from -6 to 6
- wavenumber: float32 [16, 1024, 192], P('layer', 'row'), may hold values from 0.25 to 1.5
- inverse: bfloat16 [2, 2, 3072, 3072], P(None, 'layer', 'row'), may hold values from -3 to 3
Outputs:
- preconditioned: float32 [2, 2, 16, 1024, 192], P(None, None, 'layer', 'row')
The draws below stay inside these ranges and needn't reach their ends.
All inputs are finite; a program needn't handle non-finite values.
Results may differ from the reference program's by a relative error of at most 0.003.
Values may be sent and summed in bfloat16 or wider, within the bound.
A program may use at most 64 MiB of HBM per device.

```python
import math
import jax
import jax.numpy as jnp
from jax import lax

SHOTS = 2
CZ = 8
NX = 192
QY = 16
PX = 4
SWEEPS = 4
LAYERS = 2
NZ = 16
NY = 1024
ORDER = 3072
N_LAYER = 2


def draw_inverse(key, part):
    diagonal_key, spread_key = jax.random.split(jax.random.fold_in(key, 17))
    spread = jax.random.normal(spread_key, (2, LAYERS, ORDER, ORDER), jnp.float32) * (0.35 / math.sqrt(ORDER))
    diagonal = jnp.exp(jax.random.uniform(diagonal_key, (LAYERS, ORDER), jnp.float32, math.log(1.5), math.log(2.5)))
    identity = jnp.eye(ORDER, dtype=jnp.float32)
    real_part = spread[0] + diagonal[:, :, None] * identity[None]
    return jnp.stack([real_part, spread[1]]).astype(jnp.bfloat16)


def levels(rng, extent, pieces, least, top_value):
    factor_of, own = 1.0, jax.random.fold_in(rng, 6)
    for axis_at, blocks in pieces:
        heights = jnp.exp(jax.random.uniform(jax.random.fold_in(own, axis_at), (blocks,), jnp.float32, least / len(pieces), top_value / len(pieces)))
        factor_of = factor_of * jnp.repeat(heights, extent[axis_at] // blocks).reshape([-1 if axis == axis_at else 1 for axis in range(len(extent))])
    return factor_of


def centred(key, shape, scale, most, cuts=(), kind=jnp.bfloat16):
    entries = jax.random.normal(key, shape, jnp.float32) * scale
    if len(cuts) > 0:
        entries = levels(key, shape, cuts, -0.22, 0.18) * entries
    return jnp.clip(entries, min=-most, max=most).astype(kind)


def setup_inputs(seed: int = 0) -> dict:
    seeds = jax.random.split(jax.random.key(seed), 4)
    return {
        "residual": centred(seeds[0], (SHOTS, 2, NZ, NY, NX), 1.0, 6.0, ((2, 2), (3, 16)), jnp.float32),
        "wavenumber": jnp.clip(jnp.exp(math.log(1.5) - 1.7917595 * jax.random.uniform(seeds[1], (NZ, NY, NX), jnp.float32) ** levels(seeds[1], (NZ, NY, NX), ((0, 2), (1, 16)), -0.2, 0.2)), 0.25, 1.5),
        "inverse": draw_inverse(jax.random.fold_in(seeds[3], 71), 0),
    }


damping = 0.8
absorb = 0.5
coupling = 0.45


def diagonal_parts(wavenumber):
    real_part = 6.0 - wavenumber
    imag_part = -absorb * wavenumber
    modulus = real_part * real_part + imag_part * imag_part
    return real_part, imag_part, real_part / modulus, -imag_part / modulus


def first_sweep(source, reciprocal_re, reciprocal_im):
    update_re = reciprocal_re * source[:, 0] - reciprocal_im * source[:, 1]
    update_im = reciprocal_re * source[:, 1] + reciprocal_im * source[:, 0]
    return damping * jnp.stack([update_re, update_im], axis=1)


def relax(extended, source, diagonal_re, diagonal_im, reciprocal_re, reciprocal_im):
    centre = extended[:, :, 1:-1, 1:-1, :]
    beside = extended[:, :, 2:, 1:-1, :] + extended[:, :, :-2, 1:-1, :]
    beside = beside + extended[:, :, 1:-1, 2:, :] + extended[:, :, 1:-1, :-2, :]
    padded = jnp.pad(centre, ((0, 0), (0, 0), (0, 0), (0, 0), (1, 1)))
    beside = beside + padded[..., 2:] + padded[..., :-2]
    applied_re = diagonal_re * centre[:, 0] - diagonal_im * centre[:, 1] - beside[:, 0]
    applied_im = diagonal_re * centre[:, 1] + diagonal_im * centre[:, 0] - beside[:, 1]
    remain_re = source[:, 0] - applied_re
    remain_im = source[:, 1] - applied_im
    update_re = reciprocal_re * remain_re - reciprocal_im * remain_im
    update_im = reciprocal_re * remain_im + reciprocal_im * remain_re
    return centre + damping * jnp.stack([update_re, update_im], axis=1)


def reference(residual, wavenumber, inverse):
    diagonal_re, diagonal_im, reciprocal_re, reciprocal_im = diagonal_parts(wavenumber)
    coarse_rhs = residual.reshape(SHOTS, 2, N_LAYER, CZ, NY // QY, QY, NX // PX, PX).mean(axis=(3, 5, 7))
    coarse_rhs = coarse_rhs.reshape(SHOTS, 2, N_LAYER, ORDER).transpose(2, 1, 0, 3)

    def layer_step(previous, item):
        matrices, right_side = item
        vector = (right_side + coupling * previous).astype(jnp.bfloat16)
        columns = vector.reshape(2 * SHOTS, ORDER).T
        product_re = jnp.dot(matrices[0], columns, preferred_element_type=jnp.float32).T.reshape(2, SHOTS, ORDER)
        product_im = jnp.dot(matrices[1], columns, preferred_element_type=jnp.float32).T.reshape(2, SHOTS, ORDER)
        solved = jnp.stack([product_re[0] - product_im[1], product_re[1] + product_im[0]])
        return solved, solved

    start_state = jnp.zeros((2, SHOTS, ORDER), jnp.float32)
    _, coarse_all = lax.scan(layer_step, start_state, (jnp.moveaxis(inverse, 1, 0), coarse_rhs))
    coarse_shots = coarse_all.reshape(N_LAYER, 2, SHOTS, NY // QY, NX // PX).transpose(2, 1, 0, 3, 4)

    def smooth_one(pair):
        shot_field, shot_coarse = pair
        source = shot_field[None]
        iterate = first_sweep(source, reciprocal_re, reciprocal_im)
        for counter in range(SWEEPS - 1):
            extended = jnp.pad(iterate, ((0, 0), (0, 0), (1, 1), (1, 1), (0, 0)))
            iterate = relax(extended, source, diagonal_re, diagonal_im, reciprocal_re, reciprocal_im)
        lifted = jnp.broadcast_to(shot_coarse[:, :, None, :, None, :, None], (2, N_LAYER, CZ, NY // QY, QY, NX // PX, PX))
        lifted = lifted.reshape(2, N_LAYER * CZ, NY, NX)
        return iterate[0] + lifted

    return lax.map(smooth_one, (residual, coarse_shots))
```

```python
import functools

import jax
import jax.numpy as jnp
from jax import lax
from jax.experimental import pallas as pl
from jax.experimental.pallas import tpu as pltpu
from jax.sharding import PartitionSpec as P

QY = 16
PX = 4
SWEEPS = 4

damping = 0.8
absorb = 0.5
coupling = 0.45

LANES = 128
SUB = 8
TOP = 8
MESH = pl.DeviceIdType.MESH
f32 = jnp.float32
bf16 = jnp.bfloat16


def split_rows(value):
    upper = value.astype(bf16).astype(f32)
    return jnp.concatenate([upper, value - upper], axis=0).astype(bf16)


def kernel(n_layer, n_row, res_hbm, wav_hbm, inv_hbm, out_hbm, lift_ref,
           res, wav, mat, place, recip, smooth, final, pool, gath, cgath, piece_buf, coarse_buf,
           ysend, yrecv, load_sem, gs_sem, gr_sem, cs_sem, cr_sem, zs_sem, zr_sem, ys_sem, yr_sem, out_sem):
    layer = lax.axis_index("layer")
    row = lax.axis_index("row")
    fields, depth, height, width = res.shape
    shots = fields // 2
    chunks = smooth.shape[3]
    wide = chunks * LANES
    tiles = height // SUB
    yblocks = height // QY
    xblocks = width // PX
    piece = yblocks * xblocks
    tail = width - (chunks - 1) * LANES

    load_res = pltpu.make_async_copy(res_hbm, res, load_sem.at[0])
    load_wav = pltpu.make_async_copy(wav_hbm, wav, load_sem.at[1])
    load_mat = pltpu.make_async_copy(inv_hbm, mat, load_sem.at[2])
    load_res.start()
    load_wav.start()
    load_mat.start()

    barrier = pltpu.get_barrier_semaphore()

    @pl.loop(1, n_row)
    def _(step):
        pl.semaphore_signal(barrier, inc=1, device_id=(layer, lax.rem(row + step, n_row)), device_id_type=MESH)

    @pl.when(layer < n_layer - 1)
    def _():
        @pl.loop(0, n_row)
        def _(target):
            pl.semaphore_signal(barrier, inc=1, device_id=(layer + 1, target), device_id_type=MESH)

    @pl.when(layer > 0)
    def _():
        @pl.loop(0, n_row)
        def _(target):
            pl.semaphore_signal(barrier, inc=1, device_id=(layer - 1, target), device_id_type=MESH)

    across = lax.broadcasted_iota(jnp.int32, (wide, wide), 0)
    cell = lax.broadcasted_iota(jnp.int32, (wide, wide), 1)
    for yc in range(yblocks):
        offset = across - PX * (cell - yc * xblocks)
        place[yc] = jnp.where((offset >= 0) & (offset < PX), 1.0, 0.0).astype(bf16)

    def widened(value):
        if value.shape[1] == LANES:
            return value
        return jnp.concatenate([value, jnp.zeros((value.shape[0], LANES - value.shape[1]), value.dtype)], axis=1)

    def part(ref, index, first, chunk):
        stop = min(width, (chunk + 1) * LANES)
        return widened(ref[(*index, pl.ds(first, SUB), pl.ds(chunk * LANES, stop - chunk * LANES))])

    load_res.wait()

    @pl.loop(0, yblocks)
    def _(yc):
        first = pl.multiple_of(yc * QY, QY)
        for field in range(fields):
            for chunk in range(chunks):
                stop = min(width, (chunk + 1) * LANES)
                total = None
                for z in range(depth):
                    for y in range(QY // SUB):
                        item = res[field, z, pl.ds(first + y * SUB, SUB), pl.ds(chunk * LANES, stop - chunk * LANES)]
                        total = item if total is None else total + item
                pool[yc, pl.ds(field, 1), pl.ds(chunk * LANES, LANES)] = widened(jnp.sum(total, axis=0, keepdims=True))

    summed = None
    for yc in range(yblocks):
        product = jnp.dot(split_rows(pool[yc]), place[yc], preferred_element_type=f32)
        summed = product if summed is None else summed + product
    own = (summed[:fields] + summed[fields:]) * (1.0 / (depth * QY * PX))
    shift = lax.rem(row * piece, LANES)
    own = pltpu.roll(own, shift, 1)
    piece_buf[...] = own
    gath[row] = own

    count = (n_row - 1) + jnp.where(layer < n_layer - 1, n_row, 0) + jnp.where(layer > 0, n_row, 0)
    pl.semaphore_wait(barrier, count)

    def gather_copy(target, slot_send, slot_recv):
        return pltpu.make_async_remote_copy(
            src_ref=piece_buf, dst_ref=gath.at[slot_recv], send_sem=gs_sem.at[slot_send], recv_sem=gr_sem.at[slot_recv],
            device_id=(layer, target), device_id_type=MESH)

    @pl.loop(1, n_row)
    def _(step):
        target = lax.rem(row + step, n_row)
        gather_copy(target, target, row).start()

    load_wav.wait()

    @pl.loop(0, depth)
    def _(z):
        for tile in range(tiles):
            rows = pl.ds(tile * SUB, SUB)
            for chunk in range(chunks):
                wave = part(wav, (z,), tile * SUB, chunk)
                real = 6.0 - wave
                imag = absorb * wave
                scale = damping / (real * real + imag * imag)
                g_re = real * scale
                g_im = imag * scale
                if chunk == chunks - 1 and tail < LANES:
                    inside = lax.broadcasted_iota(jnp.int32, (SUB, LANES), 1) < tail
                    g_re = jnp.where(inside, g_re, 0.0)
                    g_im = jnp.where(inside, g_im, 0.0)
                recip[0, z, chunk, rows, :] = g_re
                recip[1, z, chunk, rows, :] = g_im
                for shot in range(shots):
                    r_re = part(res, (2 * shot, z), tile * SUB, chunk)
                    r_im = part(res, (2 * shot + 1, z), tile * SUB, chunk)
                    inner = pl.ds(TOP + tile * SUB, SUB)
                    smooth[0, 2 * shot, z + 1, chunk, inner, :] = g_re * r_re - g_im * r_im
                    smooth[0, 2 * shot + 1, z + 1, chunk, inner, :] = g_re * r_im + g_im * r_re

    inner_rows = pl.ds(TOP, height)

    def z_copy(k, way):
        source, target = ((depth, 0), (1, depth + 1))[way]
        return pltpu.make_async_remote_copy(
            src_ref=smooth.at[k, :, source, :, inner_rows, :], dst_ref=smooth.at[k, :, target, :, inner_rows, :],
            send_sem=zs_sem.at[k, way], recv_sem=zr_sem.at[k, way],
            device_id=(layer + (1, -1)[way], row), device_id_type=MESH)

    def y_copy(k, way):
        return pltpu.make_async_remote_copy(
            src_ref=ysend.at[k, way], dst_ref=yrecv.at[k, way],
            send_sem=ys_sem.at[k, way], recv_sem=yr_sem.at[k, way],
            device_id=(layer, row + (1, -1)[way]), device_id_type=MESH)

    has_next = {"z": layer < n_layer - 1, "y": row < n_row - 1}
    has_last = {"z": layer > 0, "y": row > 0}

    def send_halo(k):
        for way, able in ((0, has_next["z"]), (1, has_last["z"])):
            @pl.when(able)
            def _():
                z_copy(k, way).start()

        @pl.loop(0, fields)
        def _(field):
            for z in range(depth):
                for chunk in range(chunks):
                    ysend[k, 0, field, chunk, pl.ds(z, 1), :] = smooth[k, field, z + 1, chunk, pl.ds(TOP + height - 1, 1), :]
                    ysend[k, 1, field, chunk, pl.ds(z, 1), :] = smooth[k, field, z + 1, chunk, pl.ds(TOP, 1), :]

        for way, able in ((0, has_next["y"]), (1, has_last["y"])):
            @pl.when(able)
            def _():
                y_copy(k, way).start()

    for way, able in ((0, has_last["z"]), (1, has_next["z"])):
        @pl.when(jnp.logical_not(able))
        def _():
            for k in range(SWEEPS - 1):
                @pl.loop(0, fields)
                def _(field):
                    for chunk in range(chunks):
                        smooth[k, field, (0, depth + 1)[way], chunk, inner_rows, :] = jnp.zeros((height, LANES), f32)
    for way, able in ((0, has_last["y"]), (1, has_next["y"])):
        @pl.when(jnp.logical_not(able))
        def _():
            for k in range(SWEEPS - 1):
                yrecv[k, way] = jnp.zeros(yrecv.shape[2:], f32)

    def take_halo(k):
        for way, z_able, y_able in ((0, has_last["z"], has_last["y"]), (1, has_next["z"], has_next["y"])):
            @pl.when(z_able)
            def _():
                z_copy(k, way).wait_recv()

            @pl.when(y_able)
            def _():
                y_copy(k, way).wait_recv()

        @pl.loop(0, fields)
        def _(field):
            for z in range(depth):
                for chunk in range(chunks):
                    smooth[k, field, z + 1, chunk, pl.ds(TOP - 1, 1), :] = yrecv[k, 0, field, chunk, pl.ds(z, 1), :]
                    smooth[k, field, z + 1, chunk, pl.ds(TOP + height, 1), :] = yrecv[k, 1, field, chunk, pl.ds(z, 1), :]

    def sweep(k):
        last = k == SWEEPS - 2
        lane = lax.broadcasted_iota(jnp.int32, (SUB, LANES), 1)
        first_lane, last_lane = lane == 0, lane == LANES - 1

        @pl.loop(0, depth * shots)
        def _(index):
            z = lax.div(index, shots)
            shot = lax.rem(index, shots)
            for tile in range(tiles):
                y0 = TOP + tile * SUB
                beside, centre = [], []
                for p in range(2):
                    field = 2 * shot + p
                    mid = [smooth[k, field, z + 1, c, pl.ds(y0, SUB), :] for c in range(chunks)]
                    up = [pltpu.roll(m, 1, 1) for m in mid]
                    down = [pltpu.roll(m, LANES - 1, 1) for m in mid]
                    sums = []
                    for c in range(chunks):
                        total = (smooth[k, field, z, c, pl.ds(y0, SUB), :] + smooth[k, field, z + 2, c, pl.ds(y0, SUB), :]) + (
                            smooth[k, field, z + 1, c, pl.ds(y0 - 1, SUB), :] + smooth[k, field, z + 1, c, pl.ds(y0 + 1, SUB), :])
                        before = jnp.where(first_lane, up[c - 1], up[c])
                        after = jnp.where(last_lane, down[c + 1], down[c]) if c < chunks - 1 else down[c]
                        sums.append(total + (before + after))
                    beside.append(sums)
                    centre.append(mid)
                for c in range(chunks):
                    g_re = recip[0, z, c, pl.ds(tile * SUB, SUB), :]
                    g_im = recip[1, z, c, pl.ds(tile * SUB, SUB), :]
                    moved = (g_re * beside[0][c] - g_im * beside[1][c], g_re * beside[1][c] + g_im * beside[0][c])
                    for p in range(2):
                        field = 2 * shot + p
                        value = (1.0 - damping) * centre[p][c] + moved[p]
                        value = value + (centre[p][c] if k == 0 else smooth[0, field, z + 1, c, pl.ds(y0, SUB), :])
                        if last:
                            stop = min(width, (c + 1) * LANES) - c * LANES
                            final[field, z, pl.ds(tile * SUB, SUB), pl.ds(c * LANES, stop)] = value[:, :stop]
                        else:
                            smooth[k + 1, field, z + 1, c, pl.ds(y0, SUB), :] = value

    def coarse_copy(target, slot_send, slot_recv):
        return pltpu.make_async_remote_copy(
            src_ref=coarse_buf, dst_ref=cgath.at[slot_recv], send_sem=cs_sem.at[slot_send], recv_sem=cr_sem.at[slot_recv],
            device_id=(layer + 1, target), device_id_type=MESH)

    def wait_gather():
        @pl.loop(1, n_row)
        def _(step):
            source = lax.rem(row + step, n_row)
            gather_copy(source, source, source).wait_recv()

    def solve(fed):
        parts = [None] * (mat.shape[2] // LANES)
        for source in range(n_row):
            value = gath[source]
            if fed:
                value = value + coupling * cgath[source]
            start = source * piece // LANES
            for c in range(chunks):
                if start + c < len(parts):
                    item = value[:, c * LANES:(c + 1) * LANES]
                    parts[start + c] = item if parts[start + c] is None else parts[start + c] + item
        vector = jnp.concatenate(parts, axis=1).astype(bf16)
        dims = (((1,), (1,)), ((), ()))
        by_re = lax.dot_general(vector, mat[0], dims, preferred_element_type=f32)
        by_im = lax.dot_general(vector, mat[1], dims, preferred_element_type=f32)
        rows = []
        for shot in range(shots):
            a, b = 2 * shot, 2 * shot + 1
            rows.append(by_re[a:a + 1] - by_im[b:b + 1])
            rows.append(by_re[b:b + 1] + by_im[a:a + 1])
        coarse = jnp.concatenate(rows, axis=0)
        coarse = jnp.concatenate([coarse, jnp.zeros((fields, wide - piece), f32)], axis=1)
        coarse_buf[...] = pltpu.roll(coarse, shift, 1)

        @pl.when(layer < n_layer - 1)
        def _():
            @pl.loop(0, n_row)
            def _(step):
                target = lax.rem(row + step, n_row)
                coarse_copy(target, target, row).start()

        halves = split_rows(coarse)
        for yc in range(yblocks):
            raised = lax.dot_general(halves, place[yc], dims, preferred_element_type=f32)
            raised = raised[:fields] + raised[fields:]
            for field in range(fields):
                lift_ref[field, pl.ds(yc, 1), :] = raised[field:field + 1]

    send_halo(0)

    @pl.when(layer == 0)
    def _():
        load_mat.wait()
        wait_gather()
        solve(False)

    for k in range(SWEEPS - 1):
        take_halo(k)
        sweep(k)
        if k < SWEEPS - 2:
            send_halo(k + 1)

    store = pltpu.make_async_copy(final, out_hbm, out_sem)
    store.start()

    @pl.when(layer > 0)
    def _():
        load_mat.wait()
        wait_gather()

        @pl.loop(0, n_row)
        def _(step):
            source = lax.rem(row + step, n_row)
            coarse_copy(source, source, source).wait_recv()

        solve(True)

    store.wait()

    @pl.loop(1, n_row)
    def _(step):
        target = lax.rem(row + step, n_row)
        gather_copy(target, target, target).wait_send()

    @pl.when(layer < n_layer - 1)
    def _():
        @pl.loop(0, n_row)
        def _(target):
            coarse_copy(target, target, target).wait_send()

    for k in range(SWEEPS - 1):
        for way, z_able, y_able in ((0, has_next["z"], has_next["y"]), (1, has_last["z"], has_last["y"])):
            @pl.when(z_able)
            def _():
                z_copy(k, way).wait_send()

            @pl.when(y_able)
            def _():
                y_copy(k, way).wait_send()


def on_device(residual, wavenumber, inverse):
    n_layer, n_row = lax.axis_size("layer"), lax.axis_size("row")
    shots, _, depth, height, width = residual.shape
    fields = 2 * shots
    chunks = pl.cdiv(width, LANES)
    wide = chunks * LANES
    yblocks = height // QY
    _, _, rows, order = inverse.shape
    sweeps = SWEEPS - 1
    dma = pltpu.SemaphoreType.DMA
    smoothed, lifted = pl.pallas_call(
        functools.partial(kernel, n_layer, n_row),
        out_shape=(jax.ShapeDtypeStruct((fields, depth, height, width), f32),
                   jax.ShapeDtypeStruct((fields, yblocks, wide), f32)),
        in_specs=[pl.BlockSpec(memory_space=pl.ANY)] * 3,
        out_specs=(pl.BlockSpec(memory_space=pl.ANY), pl.BlockSpec(memory_space=pltpu.VMEM)),
        scratch_shapes=[
            pltpu.VMEM((fields, depth, height, width), f32),
            pltpu.VMEM((depth, height, width), f32),
            pltpu.VMEM((2, rows, order), bf16),
            pltpu.VMEM((yblocks, wide, wide), bf16),
            pltpu.VMEM((2, depth, chunks, height, LANES), f32),
            pltpu.VMEM((sweeps, fields, depth + 2, chunks, height + 2 * TOP, LANES), f32),
            pltpu.VMEM((fields, depth, height, width), f32),
            pltpu.VMEM((yblocks, fields, wide), f32),
            pltpu.VMEM((n_row, fields, wide), f32),
            pltpu.VMEM((n_row, fields, wide), f32),
            pltpu.VMEM((fields, wide), f32),
            pltpu.VMEM((fields, wide), f32),
            pltpu.VMEM((sweeps, 2, fields, chunks, depth, LANES), f32),
            pltpu.VMEM((sweeps, 2, fields, chunks, depth, LANES), f32),
            dma((3,)), dma((n_row,)), dma((n_row,)), dma((n_row,)), dma((n_row,)),
            dma((sweeps, 2)), dma((sweeps, 2)), dma((sweeps, 2)), dma((sweeps, 2)), dma,
        ],
        compiler_params=pltpu.CompilerParams(
            collective_id=0, has_side_effects=True, vmem_limit_bytes=40 * 1024 * 1024),
    )(residual.reshape(fields, depth, height, width), wavenumber, inverse.reshape(2, rows, order))
    lifted = lifted[:, :, :width].reshape(shots, 2, 1, yblocks, 1, width)
    smoothed = smoothed.reshape(shots, 2, depth, yblocks, QY, width)
    return (smoothed + lifted).reshape(residual.shape)


def solution(mesh):
    return jax.shard_map(
        on_device,
        mesh=mesh,
        in_specs=(
            P(None, None, "layer", "row", None),
            P("layer", "row", None),
            P(None, "layer", "row", None),
        ),
        out_specs=P(None, None, "layer", "row", None),
        check_vma=False,
    )
```

```python
import functools

import jax
import jax.numpy as jnp
from jax import lax
from jax.experimental import pallas as pl
from jax.experimental.pallas import tpu as pltpu
from jax.sharding import PartitionSpec as P

QY = 16
PX = 4
SWEEPS = 4

damping = 0.8
absorb = 0.5
coupling = 0.45

LANES = 128
SUB = 8
TOP = 8
MESH = pl.DeviceIdType.MESH
f32 = jnp.float32
bf16 = jnp.bfloat16


def split_rows(value):
    upper = value.astype(bf16).astype(f32)
    return jnp.concatenate([upper, value - upper], axis=0).astype(bf16)


def kernel(n_layer, n_row, res_hbm, wav_hbm, inv_hbm, out_hbm, lift_ref,
           res, wav, mat, place, recip, smooth, final, pool, gath, cgath, piece_buf, coarse_buf,
           ysend, yrecv, load_sem, gs_sem, gr_sem, cs_sem, cr_sem, zs_sem, zr_sem, ys_sem, yr_sem, out_sem):
    layer = lax.axis_index("layer")
    row = lax.axis_index("row")
    fields, depth, height, width = res.shape
    shots = fields // 2
    chunks = smooth.shape[3]
    wide = chunks * LANES
    tiles = height // SUB
    yblocks = height // QY
    xblocks = width // PX
    piece = yblocks * xblocks
    tail = width - (chunks - 1) * LANES

    load_res = pltpu.make_async_copy(res_hbm, res, load_sem.at[0])
    load_wav = pltpu.make_async_copy(wav_hbm, wav, load_sem.at[1])
    load_mat = pltpu.make_async_copy(inv_hbm, mat, load_sem.at[2])
    load_res.start()
    load_wav.start()

    barrier = pltpu.get_barrier_semaphore()

    @pl.loop(1, n_row)
    def _(step):
        pl.semaphore_signal(barrier, inc=1, device_id=(layer, lax.rem(row + step, n_row)), device_id_type=MESH)

    @pl.when(layer < n_layer - 1)
    def _():
        @pl.loop(0, n_row)
        def _(target):
            pl.semaphore_signal(barrier, inc=1, device_id=(layer + 1, target), device_id_type=MESH)

    @pl.when(layer > 0)
    def _():
        @pl.loop(0, n_row)
        def _(target):
            pl.semaphore_signal(barrier, inc=1, device_id=(layer - 1, target), device_id_type=MESH)

    across = lax.broadcasted_iota(jnp.int32, (wide, wide), 0)
    cell = lax.broadcasted_iota(jnp.int32, (wide, wide), 1)
    for yc in range(yblocks):
        offset = across - PX * (cell - yc * xblocks)
        place[yc] = jnp.where((offset >= 0) & (offset < PX), 1.0, 0.0).astype(bf16)

    def widened(value):
        if value.shape[1] == LANES:
            return value
        return jnp.concatenate([value, jnp.zeros((value.shape[0], LANES - value.shape[1]), value.dtype)], axis=1)

    def part(ref, index, first, chunk):
        stop = min(width, (chunk + 1) * LANES)
        return widened(ref[(*index, pl.ds(first, SUB), pl.ds(chunk * LANES, stop - chunk * LANES))])

    inner_rows = pl.ds(TOP, height)
    has_next = {"z": layer < n_layer - 1, "y": row < n_row - 1}
    has_last = {"z": layer > 0, "y": row > 0}

    for way, able in ((0, has_last["z"]), (1, has_next["z"])):
        @pl.when(jnp.logical_not(able))
        def _():
            for k in range(SWEEPS - 1):
                @pl.loop(0, fields)
                def _(field):
                    for chunk in range(chunks):
                        smooth[k, field, (0, depth + 1)[way], chunk, inner_rows, :] = jnp.zeros((height, LANES), f32)
    for way, able in ((0, has_last["y"]), (1, has_next["y"])):
        @pl.when(jnp.logical_not(able))
        def _():
            for k in range(SWEEPS - 1):
                yrecv[k, way] = jnp.zeros(yrecv.shape[2:], f32)

    load_res.wait()
    load_mat.start()

    @pl.loop(0, yblocks)
    def _(yc):
        first = pl.multiple_of(yc * QY, QY)
        for field in range(fields):
            for chunk in range(chunks):
                stop = min(width, (chunk + 1) * LANES)
                total = None
                for z in range(depth):
                    for y in range(QY // SUB):
                        item = res[field, z, pl.ds(first + y * SUB, SUB), pl.ds(chunk * LANES, stop - chunk * LANES)]
                        total = item if total is None else total + item
                pool[yc, pl.ds(field, 1), pl.ds(chunk * LANES, LANES)] = widened(jnp.sum(total, axis=0, keepdims=True))

    summed = None
    for yc in range(yblocks):
        product = jnp.dot(split_rows(pool[yc]), place[yc], preferred_element_type=f32)
        summed = product if summed is None else summed + product
    own = (summed[:fields] + summed[fields:]) * (1.0 / (depth * QY * PX))
    shift = lax.rem(row * piece, LANES)
    own = pltpu.roll(own, shift, 1)
    piece_buf[...] = own
    gath[row] = own

    count = (n_row - 1) + jnp.where(layer < n_layer - 1, n_row, 0) + jnp.where(layer > 0, n_row, 0)
    pl.semaphore_wait(barrier, count)

    def gather_copy(target, slot_send, slot_recv):
        return pltpu.make_async_remote_copy(
            src_ref=piece_buf, dst_ref=gath.at[slot_recv], send_sem=gs_sem.at[slot_send], recv_sem=gr_sem.at[slot_recv],
            device_id=(layer, target), device_id_type=MESH)

    @pl.loop(1, n_row)
    def _(step):
        target = lax.rem(row + step, n_row)
        gather_copy(target, target, row).start()

    load_wav.wait()

    @pl.loop(0, depth)
    def _(z):
        for tile in range(tiles):
            rows = pl.ds(tile * SUB, SUB)
            for chunk in range(chunks):
                wave = part(wav, (z,), tile * SUB, chunk)
                real = 6.0 - wave
                imag = absorb * wave
                scale = damping / (real * real + imag * imag)
                g_re = real * scale
                g_im = imag * scale
                if chunk == chunks - 1 and tail < LANES:
                    inside = lax.broadcasted_iota(jnp.int32, (SUB, LANES), 1) < tail
                    g_re = jnp.where(inside, g_re, 0.0)
                    g_im = jnp.where(inside, g_im, 0.0)
                recip[0, z, chunk, rows, :] = g_re
                recip[1, z, chunk, rows, :] = g_im
                for shot in range(shots):
                    r_re = part(res, (2 * shot, z), tile * SUB, chunk)
                    r_im = part(res, (2 * shot + 1, z), tile * SUB, chunk)
                    inner = pl.ds(TOP + tile * SUB, SUB)
                    smooth[0, 2 * shot, z + 1, chunk, inner, :] = g_re * r_re - g_im * r_im
                    smooth[0, 2 * shot + 1, z + 1, chunk, inner, :] = g_re * r_im + g_im * r_re

    def z_copy(k, way):
        source, target = ((depth, 0), (1, depth + 1))[way]
        return pltpu.make_async_remote_copy(
            src_ref=smooth.at[k, :, source, :, inner_rows, :], dst_ref=smooth.at[k, :, target, :, inner_rows, :],
            send_sem=zs_sem.at[k, way], recv_sem=zr_sem.at[k, way],
            device_id=(layer + (1, -1)[way], row), device_id_type=MESH)

    def y_copy(k, way):
        return pltpu.make_async_remote_copy(
            src_ref=ysend.at[k, way], dst_ref=yrecv.at[k, way],
            send_sem=ys_sem.at[k, way], recv_sem=yr_sem.at[k, way],
            device_id=(layer, row + (1, -1)[way]), device_id_type=MESH)

    def send_halo(k):
        for way, able in ((0, has_next["z"]), (1, has_last["z"])):
            @pl.when(able)
            def _():
                z_copy(k, way).start()

        @pl.loop(0, fields)
        def _(field):
            for z in range(depth):
                for chunk in range(chunks):
                    ysend[k, 0, field, chunk, pl.ds(z, 1), :] = smooth[k, field, z + 1, chunk, pl.ds(TOP + height - 1, 1), :]
                    ysend[k, 1, field, chunk, pl.ds(z, 1), :] = smooth[k, field, z + 1, chunk, pl.ds(TOP, 1), :]

        for way, able in ((0, has_next["y"]), (1, has_last["y"])):
            @pl.when(able)
            def _():
                y_copy(k, way).start()

    def take_halo(k):
        for way, z_able, y_able in ((0, has_last["z"], has_last["y"]), (1, has_next["z"], has_next["y"])):
            @pl.when(z_able)
            def _():
                z_copy(k, way).wait_recv()

            @pl.when(y_able)
            def _():
                y_copy(k, way).wait_recv()

        @pl.loop(0, fields)
        def _(field):
            for z in range(depth):
                for chunk in range(chunks):
                    smooth[k, field, z + 1, chunk, pl.ds(TOP - 1, 1), :] = yrecv[k, 0, field, chunk, pl.ds(z, 1), :]
                    smooth[k, field, z + 1, chunk, pl.ds(TOP + height, 1), :] = yrecv[k, 1, field, chunk, pl.ds(z, 1), :]

    def relax(k, z, shot, which):
        last = k == SWEEPS - 2
        lane = lax.broadcasted_iota(jnp.int32, (SUB, LANES), 1)
        first_lane, last_lane = lane == 0, lane == LANES - 1
        for tile in which:
            y0 = TOP + tile * SUB
            beside, centre = [], []
            for p in range(2):
                field = 2 * shot + p
                mid = [smooth[k, field, z + 1, c, pl.ds(y0, SUB), :] for c in range(chunks)]
                up = [pltpu.roll(m, 1, 1) for m in mid]
                down = [pltpu.roll(m, LANES - 1, 1) for m in mid]
                sums = []
                for c in range(chunks):
                    total = (smooth[k, field, z, c, pl.ds(y0, SUB), :] + smooth[k, field, z + 2, c, pl.ds(y0, SUB), :]) + (
                        smooth[k, field, z + 1, c, pl.ds(y0 - 1, SUB), :] + smooth[k, field, z + 1, c, pl.ds(y0 + 1, SUB), :])
                    before = jnp.where(first_lane, up[c - 1], up[c])
                    after = jnp.where(last_lane, down[c + 1], down[c]) if c < chunks - 1 else down[c]
                    sums.append(total + (before + after))
                beside.append(sums)
                centre.append(mid)
            for c in range(chunks):
                g_re = recip[0, z, c, pl.ds(tile * SUB, SUB), :]
                g_im = recip[1, z, c, pl.ds(tile * SUB, SUB), :]
                moved = (g_re * beside[0][c] - g_im * beside[1][c], g_re * beside[1][c] + g_im * beside[0][c])
                for p in range(2):
                    field = 2 * shot + p
                    value = (1.0 - damping) * centre[p][c] + moved[p]
                    value = value + (centre[p][c] if k == 0 else smooth[0, field, z + 1, c, pl.ds(y0, SUB), :])
                    if last:
                        stop = min(width, (c + 1) * LANES) - c * LANES
                        final[field, z, pl.ds(tile * SUB, SUB), pl.ds(c * LANES, stop)] = value[:, :stop]
                    else:
                        smooth[k + 1, field, z + 1, c, pl.ds(y0, SUB), :] = value

    def inside(k):
        @pl.loop(0, (depth - 2) * shots)
        def _(index):
            relax(k, 1 + lax.div(index, shots), lax.rem(index, shots), range(1, tiles - 1))

    def rim(k):
        @pl.loop(0, 2 * shots)
        def _(index):
            relax(k, lax.div(index, shots) * (depth - 1), lax.rem(index, shots), range(tiles))

        @pl.loop(0, (depth - 2) * shots)
        def _(index):
            relax(k, 1 + lax.div(index, shots), lax.rem(index, shots), (0, tiles - 1))

    def coarse_copy(target, slot_send, slot_recv):
        return pltpu.make_async_remote_copy(
            src_ref=coarse_buf, dst_ref=cgath.at[slot_recv], send_sem=cs_sem.at[slot_send], recv_sem=cr_sem.at[slot_recv],
            device_id=(layer + 1, target), device_id_type=MESH)

    def wait_gather():
        @pl.loop(1, n_row)
        def _(step):
            source = lax.rem(row + step, n_row)
            gather_copy(source, source, source).wait_recv()

    def solve(fed):
        parts = [None] * (mat.shape[2] // LANES)
        for source in range(n_row):
            value = gath[source]
            if fed:
                value = value + coupling * cgath[source]
            start = source * piece // LANES
            for c in range(chunks):
                if start + c < len(parts):
                    item = value[:, c * LANES:(c + 1) * LANES]
                    parts[start + c] = item if parts[start + c] is None else parts[start + c] + item
        vector = jnp.concatenate(parts, axis=1).astype(bf16)
        dims = (((1,), (1,)), ((), ()))
        by_re = lax.dot_general(vector, mat[0], dims, preferred_element_type=f32)
        by_im = lax.dot_general(vector, mat[1], dims, preferred_element_type=f32)
        rows = []
        for shot in range(shots):
            a, b = 2 * shot, 2 * shot + 1
            rows.append(by_re[a:a + 1] - by_im[b:b + 1])
            rows.append(by_re[b:b + 1] + by_im[a:a + 1])
        coarse = jnp.concatenate(rows, axis=0)
        coarse = jnp.concatenate([coarse, jnp.zeros((fields, wide - piece), f32)], axis=1)
        coarse_buf[...] = pltpu.roll(coarse, shift, 1)

        @pl.when(layer < n_layer - 1)
        def _():
            @pl.loop(0, n_row)
            def _(step):
                target = lax.rem(row + step, n_row)
                coarse_copy(target, target, row).start()

        halves = split_rows(coarse)
        for yc in range(yblocks):
            raised = lax.dot_general(halves, place[yc], dims, preferred_element_type=f32)
            raised = raised[:fields] + raised[fields:]
            for field in range(fields):
                lift_ref[field, pl.ds(yc, 1), :] = raised[field:field + 1]

    send_halo(0)
    for k in range(SWEEPS - 1):
        inside(k)
        take_halo(k)
        rim(k)
        if k < SWEEPS - 2:
            send_halo(k + 1)
        if k == 0:
            @pl.when(layer == 0)
            def _():
                load_mat.wait()
                wait_gather()
                solve(False)

    store = pltpu.make_async_copy(final, out_hbm, out_sem)
    store.start()

    @pl.when(layer > 0)
    def _():
        load_mat.wait()
        wait_gather()

        @pl.loop(0, n_row)
        def _(step):
            source = lax.rem(row + step, n_row)
            coarse_copy(source, source, source).wait_recv()

        solve(True)

    store.wait()

    @pl.loop(1, n_row)
    def _(step):
        target = lax.rem(row + step, n_row)
        gather_copy(target, target, target).wait_send()

    @pl.when(layer < n_layer - 1)
    def _():
        @pl.loop(0, n_row)
        def _(target):
            coarse_copy(target, target, target).wait_send()

    for k in range(SWEEPS - 1):
        for way, z_able, y_able in ((0, has_next["z"], has_next["y"]), (1, has_last["z"], has_last["y"])):
            @pl.when(z_able)
            def _():
                z_copy(k, way).wait_send()

            @pl.when(y_able)
            def _():
                y_copy(k, way).wait_send()


def on_device(residual, wavenumber, inverse):
    n_layer, n_row = lax.axis_size("layer"), lax.axis_size("row")
    shots, _, depth, height, width = residual.shape
    fields = 2 * shots
    chunks = pl.cdiv(width, LANES)
    wide = chunks * LANES
    yblocks = height // QY
    _, _, rows, order = inverse.shape
    sweeps = SWEEPS - 1
    dma = pltpu.SemaphoreType.DMA
    smoothed, lifted = pl.pallas_call(
        functools.partial(kernel, n_layer, n_row),
        out_shape=(jax.ShapeDtypeStruct((fields, depth, height, width), f32),
                   jax.ShapeDtypeStruct((fields, yblocks, wide), f32)),
        in_specs=[pl.BlockSpec(memory_space=pltpu.HBM)] * 3,
        out_specs=(pl.BlockSpec(memory_space=pl.ANY), pl.BlockSpec(memory_space=pltpu.VMEM)),
        scratch_shapes=[
            pltpu.VMEM((fields, depth, height, width), f32),
            pltpu.VMEM((depth, height, width), f32),
            pltpu.VMEM((2, rows, order), bf16),
            pltpu.VMEM((yblocks, wide, wide), bf16),
            pltpu.VMEM((2, depth, chunks, height, LANES), f32),
            pltpu.VMEM((sweeps, fields, depth + 2, chunks, height + 2 * TOP, LANES), f32),
            pltpu.VMEM((fields, depth, height, width), f32),
            pltpu.VMEM((yblocks, fields, wide), f32),
            pltpu.VMEM((n_row, fields, wide), f32),
            pltpu.VMEM((n_row, fields, wide), f32),
            pltpu.VMEM((fields, wide), f32),
            pltpu.VMEM((fields, wide), f32),
            pltpu.VMEM((sweeps, 2, fields, chunks, depth, LANES), f32),
            pltpu.VMEM((sweeps, 2, fields, chunks, depth, LANES), f32),
            dma((3,)), dma((n_row,)), dma((n_row,)), dma((n_row,)), dma((n_row,)),
            dma((sweeps, 2)), dma((sweeps, 2)), dma((sweeps, 2)), dma((sweeps, 2)), dma,
        ],
        compiler_params=pltpu.CompilerParams(
            collective_id=0, has_side_effects=True, vmem_limit_bytes=60 * 1024 * 1024),
    )(residual.reshape(fields, depth, height, width), wavenumber, inverse.reshape(2, rows, order))
    lifted = lifted[:, :, :width].reshape(shots, 2, 1, yblocks, 1, width)
    smoothed = smoothed.reshape(shots, 2, depth, yblocks, QY, width)
    return (smoothed + lifted).reshape(residual.shape)


def solution(mesh):
    return jax.shard_map(
        on_device,
        mesh=mesh,
        in_specs=(
            P(None, None, "layer", "row", None),
            P("layer", "row", None),
            P(None, "layer", "row", None),
        ),
        out_specs=P(None, None, "layer", "row", None),
        check_vma=False,
    )
```
